768 devices in a mesh: dp: 48 (over x, z), heads: 16 (over y, core).
Axes of the slice: x: 4, y: 8, z: 12, core: 2. Of those that a mesh axis runs over, the one named last changes fastest.
Arguments:
- patch_queries: bfloat16 [49152, 6144], P('dp', 'heads'), may hold values from -144 to 144
- patch_keys: bfloat16 [49152, 6144], P('dp', 'heads'), may hold values from -6 to 6
- patch_values: bfloat16 [49152, 6144], P('dp', 'heads'), may hold values from -6 to 6
- out_proj: bfloat16 [6144, 6144], P('heads'), may hold values from -0.625 to 0.625
- pool_grad: bfloat16 [144, 6144], P('dp', 'heads'), may hold values from -6 to 6
- image_of_slot: int32 [49152], P('dp'), may hold values from -1 to 2, as said below
Outputs:
- pooled: bfloat16 [144, 6144], P('dp', 'heads')
- query_grad: bfloat16 [49152, 6144], P('dp', 'heads')
- key_grad: bfloat16 [49152, 6144], P('dp', 'heads')
- value_grad: bfloat16 [49152, 6144], P('dp', 'heads')
The draws below stay inside these ranges and needn't reach their ends.
Inputs may be any that keep to these rules, and one draw needn't show every extreme that they name: `image_of_slot`: within a block, slot m * 256 + c (m < 1, c < 256) holds image m or -1, live slots a prefix of the 256; slot 256 + j * 384 + c (j < 2, c < 384) holds image 1 + j or -1, live slots a prefix of the 384. Only blocks of dp index below 24 hold live slots of images 1 and above; in each of them image 0 fills 256 slots, every image has live slots and image 1 fills 384; in some of them image 2 fills 384 as well.
All inputs are finite; a program needn't handle non-finite values.
Results may differ from the reference program's by a relative error of at most 0.023.
Values may be sent and summed in bfloat16 or wider, within the bound.
No kernel may reach another device: no remote copies, remote signals or barrier semaphores. Data moves between devices by JAX's collectives and lax.ppermute only.
A program may use at most 64 MiB of HBM per device.

```python
import jax
import jax.numpy as jnp
from jax import lax

D = 6144
HEADS = 48
HS = 128
STAY_LEN = 256
STAY_IMG = 1
MOVE_IMG = 2
CAP = 384
SLOTS = 1024
IMG_DEV = 3
TOKENS = 49152
IMAGES = 144
N_DP = 48


def shared_keys(key):
    return jnp.clip(jax.random.normal(key, (TOKENS, HEADS * HS), jnp.float32), -6.0, 6.0)


def draw_patch_keys(key, part):
    key_base = shared_keys(key)
    return key_base.astype(jnp.bfloat16)


def draw_patch_queries(key, part):
    key_base = shared_keys(key)
    key = jax.random.fold_in(key, 5)
    return jnp.clip(jax.random.normal(key, key_base.shape, jnp.float32), -6.0, 6.0).astype(jnp.bfloat16)


def draw_image_of_slot(key, part):
    key = jax.random.fold_in(key, 3)
    first_key, second_key, third_key = jax.random.split(key, 3)
    half_count = N_DP // 2
    device_ids = jnp.arange(N_DP)
    busy = device_ids < half_count
    stay_len = jax.random.randint(first_key, (N_DP, STAY_IMG), STAY_LEN // 4, STAY_LEN + 1)
    stay_len = stay_len.at[:, 0].set(jnp.where(busy, STAY_LEN, stay_len[:, 0]))
    keep_slot = busy[:, None] | (jnp.arange(STAY_IMG)[None, :] == 0)
    stay_len = jnp.where(keep_slot, stay_len, 0)
    move_len = jax.random.randint(second_key, (N_DP, MOVE_IMG), CAP - CAP // 4, CAP + 1)
    move_len = move_len.at[:, 0].set(CAP)
    full_device = jax.random.randint(third_key, (), 0, half_count)
    move_len = move_len.at[:, MOVE_IMG - 1].set(jnp.where(device_ids == full_device, CAP, move_len[:, MOVE_IMG - 1]))
    move_len = jnp.where(busy[:, None], move_len, 0)
    stay_pos = jnp.arange(STAY_LEN)
    stay_seg = jnp.where(stay_pos[None, None, :] < stay_len[:, :, None], jnp.arange(STAY_IMG)[None, :, None], -1)
    move_pos = jnp.arange(CAP)
    move_seg = jnp.where(move_pos[None, None, :] < move_len[:, :, None], STAY_IMG + jnp.arange(MOVE_IMG)[None, :, None], -1)
    joined = jnp.concatenate([stay_seg.reshape(N_DP, -1), move_seg.reshape(N_DP, -1)], axis=1)
    return joined.reshape(-1).astype(jnp.int32)


def shard_levels(own_key, shape, cuts, low, largest):
    def one(axis_at, blocks):
        heights = jax.random.uniform(jax.random.fold_in(jax.random.fold_in(own_key, 6), axis_at), (blocks,), jnp.float32, low / len(cuts), largest / len(cuts))
        return jnp.repeat(jnp.exp(heights), shape[axis_at] // blocks).reshape((-1,) + (1,) * (len(shape) - axis_at - 1))

    gain = one(*cuts[0])
    for cut in cuts[1:]:
        gain = gain * one(*cut)
    return gain


def gaussian(rng, shape, deviation, bound, pieces=(), kind=jnp.bfloat16):
    values = jax.random.normal(rng, shape, jnp.float32) * deviation
    if len(pieces) > 0:
        values = shard_levels(rng, shape, pieces, -0.22, 0.18) * values
    return jnp.clip(values, min=-bound, max=bound).astype(kind)


def setup_inputs(seed: int = 0) -> dict:
    streams_of = jax.random.split(jax.random.key(seed), 7)
    patch_queries = draw_patch_queries(jax.random.fold_in(streams_of[6], 71), 0)
    patch_keys = draw_patch_keys(jax.random.fold_in(streams_of[6], 71), 0)
    patch_values = gaussian(streams_of[2], (TOKENS, HEADS * HS), 1.0, 6.0, ((0, 48), (1, 16)))
    out_proj = gaussian(streams_of[3], (HEADS * HS, D), (HEADS * HS // 64) ** -0.5, 0.625, ((0, 16),))
    pool_grad = gaussian(streams_of[4], (IMAGES, D), 1.0, 6.0, ((0, 48), (1, 16)))
    image_of_slot = draw_image_of_slot(jax.random.fold_in(streams_of[6], 71), 0)
    return dict(patch_queries=patch_queries, patch_keys=patch_keys, patch_values=patch_values, out_proj=out_proj, pool_grad=pool_grad, image_of_slot=image_of_slot)


def probabilities(query_heads, key_heads, segment):
    scores = jnp.einsum('qhd,khd->hqk', query_heads, key_heads) * (HS ** -0.5)
    row_total = segment.shape[0]
    allowed = ((segment[:, None] == segment[None, :]) & (segment[:, None] >= 0)) | jnp.eye(row_total, dtype=bool)
    scores = jnp.where(allowed[None], scores, -1e30)
    scores = scores - jnp.max(scores, axis=-1, keepdims=True)
    weights = jnp.exp(scores)
    return weights / jnp.sum(weights, axis=-1, keepdims=True)


def tile_pass(block):
    query_tile, key_tile, value_tile, segment, grad_tile = block
    row_count = query_tile.shape[0]

    def compute():
        query_heads = query_tile.astype(jnp.float32).reshape(row_count, -1, HS)
        key_heads = key_tile.astype(jnp.float32).reshape(row_count, -1, HS)
        value_heads = value_tile.astype(jnp.float32).reshape(row_count, -1, HS)
        grad_heads = grad_tile.astype(jnp.float32).reshape(row_count, -1, HS)
        prob = probabilities(query_heads, key_heads, segment)
        rounded = lax.optimization_barrier(prob.astype(jnp.bfloat16))
        weights = rounded.astype(jnp.float32)
        attended = jnp.einsum('hqk,khd->qhd', weights, value_heads).astype(jnp.bfloat16)
        value_grad = jnp.einsum('hqk,qhd->khd', weights, grad_heads).astype(jnp.bfloat16)
        prob_grad = jnp.einsum('qhd,khd->hqk', grad_heads, value_heads)
        delta = jnp.sum(prob * prob_grad, axis=-1, keepdims=True)
        score_round = lax.optimization_barrier((prob * (prob_grad - delta) * (HS ** -0.5)).astype(jnp.bfloat16))
        score_grad = score_round.astype(jnp.float32)
        query_grad = jnp.einsum('hqk,khd->qhd', score_grad, key_heads).astype(jnp.bfloat16)
        key_grad = jnp.einsum('hqk,qhd->khd', score_grad, query_heads).astype(jnp.bfloat16)
        return (attended.reshape(row_count, -1), query_grad.reshape(row_count, -1),
                key_grad.reshape(row_count, -1), value_grad.reshape(row_count, -1))

    def skipped():
        empty = jnp.zeros(query_tile.shape, jnp.bfloat16)
        return (empty, empty, empty, empty)

    return lax.cond(jnp.any(segment >= 0), compute, skipped)


def blockwise(arrays, row_count):
    tile_count = arrays[0].shape[0] // row_count
    shaped = tuple(array.reshape((tile_count, row_count) + array.shape[1:]) for array in arrays)
    result = lax.map(tile_pass, shaped)
    return tuple(array.reshape((tile_count * row_count,) + array.shape[2:]) for array in result)


def reference(patch_queries, patch_keys, patch_values, out_proj, pool_grad, image_of_slot):
    stay_rows = STAY_IMG * STAY_LEN
    width_all = HEADS * HS

    def one_device(block):
        queries_dev, keys_dev, values_dev, segment, grad_rows = block
        image_ids = jnp.arange(IMG_DEV, dtype=jnp.int32)
        member = segment[None, :] == image_ids[:, None]
        counts = jnp.sum(member.astype(jnp.float32), axis=1)
        divisor = jnp.maximum(counts, 1.0)[:, None]
        member_b = member.astype(jnp.bfloat16)
        image_grad = (jnp.dot(grad_rows, out_proj.T, preferred_element_type=jnp.float32) / divisor).astype(jnp.bfloat16)
        out_grad = jnp.dot(member_b.T, image_grad, preferred_element_type=jnp.float32).astype(jnp.bfloat16)
        front = blockwise((queries_dev[:stay_rows], keys_dev[:stay_rows], values_dev[:stay_rows],
                           segment[:stay_rows], out_grad[:stay_rows]), STAY_LEN)
        back = blockwise((queries_dev[stay_rows:], keys_dev[stay_rows:], values_dev[stay_rows:],
                          segment[stay_rows:], out_grad[stay_rows:]), CAP)
        joined = tuple(jnp.concatenate([first, second], axis=0) for first, second in zip(front, back))
        attended = joined[0]
        mean = (jnp.dot(member_b, attended, preferred_element_type=jnp.float32) / divisor).astype(jnp.bfloat16)
        pooled_dev = jnp.dot(mean, out_proj, preferred_element_type=jnp.float32).astype(jnp.bfloat16)
        return pooled_dev, joined[1], joined[2], joined[3]

    shaped = (patch_queries.reshape(N_DP, SLOTS, width_all), patch_keys.reshape(N_DP, SLOTS, width_all),
              patch_values.reshape(N_DP, SLOTS, width_all), image_of_slot.reshape(N_DP, SLOTS),
              pool_grad.reshape(N_DP, IMG_DEV, D))
    pooled, query_grad, key_grad, value_grad = lax.map(one_device, shaped)
    return (pooled.reshape(IMAGES, D), query_grad.reshape(TOKENS, width_all),
            key_grad.reshape(TOKENS, width_all), value_grad.reshape(TOKENS, width_all))
```

```python
import functools

import jax
import jax.numpy as jnp
from jax import lax
from jax.experimental import pallas as pl
from jax.experimental.pallas import tpu as pltpu
from jax.sharding import PartitionSpec as P

HS = 128
D = 6144
HEADS_DEV = 3
WIDTH = HEADS_DEV * HS
PEERS = 16
SLOTS = 1024
IMG_DEV = 3
STARTS = (0, 256, 640)
SIZES = (256, 384, 384)
SCALE = HS**-0.5
LOG2E = 1.4426950408889634
ROWS = 8
VMEM_LIMIT = 24 * 2**20

NT = (((1,), (1,)), ((), ()))
NN = (((1,), (0,)), ((), ()))
TN = (((0,), (0,)), ((), ()))


def dot(a, b, dims):
    return lax.dot_general(a, b, dims, preferred_element_type=jnp.float32)


def live_count(segment_ref, image):
    first, last = STARTS[image] // 128, (STARTS[image] + SIZES[image]) // 128
    live = (segment_ref[first:last, :] >= 0).astype(jnp.float32)
    return jnp.sum(live).astype(jnp.int32)


def rows_of(image):
    return pl.ds(STARTS[image], SIZES[image])


def cols_of(head):
    return pl.ds(head * HS, HS)


def probs_kernel(
    segment_hbm, grad_hbm, q_hbm, k_hbm, v_hbm, proj_hbm,
    send_ref, segment_ref, q_ref, k_ref, v_ref, proj_ref, prob0_ref, prob1_ref, prob2_ref, total_ref,
    grad_ref, mean_ref, sems,
):
    prob_refs = (prob0_ref, prob1_ref, prob2_ref)
    copies = {}
    segment_copy = pltpu.make_async_copy(segment_hbm, segment_ref, sems.at[10])
    segment_copy.start()
    for image in range(IMG_DEV):
        rows = rows_of(image)
        for at, (src, dst) in enumerate(((q_hbm, q_ref), (k_hbm, k_ref), (v_hbm, v_ref))):
            copies[image, at] = pltpu.make_async_copy(src.at[rows], dst.at[rows], sems.at[image * 3 + at])
            copies[image, at].start()
    proj_copy = pltpu.make_async_copy(proj_hbm, proj_ref, sems.at[9])
    proj_copy.start()
    grad_copy = pltpu.make_async_copy(grad_hbm, grad_ref, sems.at[11])
    grad_copy.start()
    segment_copy.wait()
    mean_ref[...] = jnp.zeros_like(mean_ref)
    for image in range(IMG_DEV):
        size, rows = SIZES[image], rows_of(image)
        live = live_count(segment_ref, image)
        divisor = jnp.maximum(live, 1).astype(jnp.float32)
        ones = jnp.ones((size, HS), jnp.bfloat16)
        live_t = lax.broadcasted_iota(jnp.int32, (1, size), 1) < live
        for at in range(3):
            copies[image, at].wait()
        for head in range(HEADS_DEV):
            cols = cols_of(head)
            scores = dot(k_ref[rows, cols], q_ref[rows, cols], NT)
            if image != 1:
                live_u = lax.broadcasted_iota(jnp.int32, (size, size), 0) < live
                scores = jnp.where(live_u, scores, -1e30)
            weights = jnp.exp2((scores - jnp.max(scores, axis=0, keepdims=True)) * (SCALE * LOG2E))
            factor = jnp.where(live_t, 1.0 / jnp.sum(weights, axis=0, keepdims=True), 0.0)
            prob = weights * factor
            prob_refs[image][head] = prob
            total = dot(prob.astype(jnp.bfloat16), ones, NN)
            total_ref[rows, cols] = total
            summed = jnp.sum(total * v_ref[rows, cols].astype(jnp.float32), axis=0, keepdims=True)
            mean_ref[pl.ds(image, 1), cols] = summed / divisor
    proj_copy.wait()
    grad_copy.wait()
    grad = grad_ref[...].astype(jnp.float32)
    held = jnp.concatenate([jnp.zeros((3, WIDTH), jnp.float32), grad, jnp.zeros((2, WIDTH), jnp.float32)], axis=0)
    mean = mean_ref[...].astype(jnp.bfloat16)
    for peer in range(PEERS):
        share = dot(mean, proj_ref[:, pl.ds(peer * WIDTH, WIDTH)], NN)
        send_ref[peer] = (share + held).astype(jnp.bfloat16)


def grads_kernel(
    got_ref, segment_ref, q_ref, k_ref, v_ref, proj_ref, prob0_ref, prob1_ref, prob2_ref, total_ref,
    pooled_ref, dq_hbm, dk_hbm, dv_hbm,
    dq_ref, dk_ref, dv_ref, sems,
):
    prob_refs = (prob0_ref, prob1_ref, prob2_ref)
    summed = jnp.zeros((ROWS, WIDTH), jnp.float32)
    pooled = jnp.zeros((ROWS, WIDTH), jnp.float32)
    for peer in range(PEERS):
        got = got_ref[peer]
        pooled += got.astype(jnp.float32)
        summed += dot(got, proj_ref[:, pl.ds(peer * WIDTH, WIDTH)], NT)
    pooled_ref[...] = pooled[:IMG_DEV].astype(jnp.bfloat16)
    copies = []
    for image in (1, 2, 0):
        size, rows = SIZES[image], rows_of(image)
        divisor = jnp.maximum(live_count(segment_ref, image), 1).astype(jnp.float32)
        for head in range(HEADS_DEV):
            cols = cols_of(head)
            grad = (summed[3 + image : 4 + image, head * HS : (head + 1) * HS] / divisor).astype(jnp.bfloat16)
            grad_f = grad.astype(jnp.float32)
            across = dot(v_ref[rows, cols], jnp.broadcast_to(grad, (HS, HS)), NT) * SCALE
            across = jnp.concatenate([across] * (size // HS), axis=1)
            prob = prob_refs[image][head]
            delta = jnp.sum(prob * across, axis=0, keepdims=True)
            score_grad = (prob * (across - delta)).astype(jnp.bfloat16)
            dk_ref[rows, cols] = dot(score_grad, q_ref[rows, cols], NN).astype(jnp.bfloat16)
            dq_ref[rows, cols] = dot(score_grad, k_ref[rows, cols], TN).astype(jnp.bfloat16)
            dv_ref[rows, cols] = (total_ref[rows, cols] * grad_f).astype(jnp.bfloat16)
        for at, (src, dst) in enumerate(((dq_ref, dq_hbm), (dk_ref, dk_hbm), (dv_ref, dv_hbm))):
            copy = pltpu.make_async_copy(src.at[rows], dst.at[rows], sems.at[image * 3 + at])
            copy.start()
            copies.append(copy)
    for copy in copies:
        copy.wait()


def in_hbm(x):
    return pltpu.with_memory_space_constraint(x, pltpu.HBM)


def on_device(patch_queries, patch_keys, patch_values, out_proj, pool_grad, image_of_slot):
    segment = image_of_slot.reshape(SLOTS // 128, 128)
    here, anywhere = pl.BlockSpec(memory_space=pltpu.VMEM), pl.BlockSpec(memory_space=pl.ANY)
    patch = (SLOTS, WIDTH)
    bf16, f32 = jnp.bfloat16, jnp.float32
    kept_shapes = (
        ((SLOTS // 128, 128), jnp.int32), (patch, bf16), (patch, bf16), (patch, bf16), ((WIDTH, D), bf16),
        *(((HEADS_DEV, size, size), f32) for size in SIZES), (patch, f32),
    )
    send, *kept = pl.pallas_call(
        probs_kernel,
        out_shape=[pltpu.VMEM((PEERS, ROWS, WIDTH), bf16)] + [pltpu.VMEM(*s) for s in kept_shapes],
        in_specs=[anywhere] * 6,
        out_specs=[here] * 10,
        scratch_shapes=[
            pltpu.VMEM((IMG_DEV, WIDTH), bf16), pltpu.VMEM((ROWS, WIDTH), f32), pltpu.SemaphoreType.DMA((12,)),
        ],
        compiler_params=pltpu.CompilerParams(vmem_limit_bytes=VMEM_LIMIT),
        name="probs",
    )(*(in_hbm(x) for x in (segment, pool_grad, patch_queries, patch_keys, patch_values, out_proj)))
    got = lax.all_to_all(send, "heads", 0, 0, tiled=False)
    grad_shape = jax.ShapeDtypeStruct(patch, bf16)
    return pl.pallas_call(
        grads_kernel,
        out_shape=[jax.ShapeDtypeStruct((IMG_DEV, WIDTH), bf16)] + [grad_shape] * 3,
        in_specs=[here] * 10,
        out_specs=[here] + [anywhere] * 3,
        scratch_shapes=[pltpu.VMEM(patch, bf16)] * 3 + [pltpu.SemaphoreType.DMA((9,))],
        compiler_params=pltpu.CompilerParams(vmem_limit_bytes=VMEM_LIMIT),
        name="grads",
    )(got, *kept)


def solution(mesh):
    in_specs = (
        P("dp", "heads"),
        P("dp", "heads"),
        P("dp", "heads"),
        P("heads", None),
        P("dp", "heads"),
        P("dp"),
    )
    out_specs = (P("dp", "heads"), P("dp", "heads"), P("dp", "heads"), P("dp", "heads"))
    return jax.shard_map(
        on_device, mesh=mesh, in_specs=in_specs, out_specs=out_specs, check_vma=False
    )
```

```python
import functools

import jax
import jax.numpy as jnp
from jax import lax
from jax.experimental import pallas as pl
from jax.experimental.pallas import tpu as pltpu
from jax.sharding import PartitionSpec as P

HS = 128
D = 6144
HEADS_DEV = 3
WIDTH = HEADS_DEV * HS
PEERS = 16
SLOTS = 1024
IMG_DEV = 3
STARTS = (0, 256, 640)
SIZES = (256, 384, 384)
SCALE = HS**-0.5
LOG2E = 1.4426950408889634
ROWS = 8
STRIP_A = 128
STRIP_B = 0
ORDER = (1, 2, 0)
VMEM_LIMIT = 24 * 2**20

NT = (((1,), (1,)), ((), ()))
NN = (((1,), (0,)), ((), ()))
TN = (((0,), (0,)), ((), ()))


def dot(a, b, dims):
    return lax.dot_general(a, b, dims, preferred_element_type=jnp.float32)


def live_count(segment_ref, image):
    first, last = STARTS[image] // 128, (STARTS[image] + SIZES[image]) // 128
    live = (segment_ref[first:last, :] >= 0).astype(jnp.float32)
    return jnp.sum(live).astype(jnp.int32)


def rows_of(image):
    return pl.ds(STARTS[image], SIZES[image])


def cols_of(head):
    return pl.ds(head * HS, HS)


def probs_kernel(
    segment_hbm, grad_hbm, q_hbm, k_hbm, v_hbm, proj_hbm,
    send_ref, segment_ref, q_ref, k_ref, v_ref, proj_ref, prob0_ref, prob1_ref, prob2_ref, total_ref,
    grad_ref, share_ref, score_ref, sems,
):
    prob_refs = (prob0_ref, prob1_ref, prob2_ref)
    copies = {}

    def fetch(key, src, dst):
        copies[key] = pltpu.make_async_copy(src, dst, sems.at[len(copies)])
        copies[key].start()

    def arrive(*keys):
        for key in keys:
            copies[key].wait()

    fetch("segment", segment_hbm, segment_ref)
    for image in range(IMG_DEV):
        rows = rows_of(image)
        for name, src, dst in (("q", q_hbm, q_ref), ("k", k_hbm, k_ref), ("v", v_hbm, v_ref)):
            fetch((name, image), src.at[rows], dst.at[rows])
    fetch("grad", grad_hbm, grad_ref)
    for head in range(HEADS_DEV):
        rows = cols_of(head)
        fetch(("proj", head), proj_hbm.at[rows], proj_ref.at[rows])
    arrive("segment")
    live = [live_count(segment_ref, image) for image in range(IMG_DEV)]

    def score(image, head):
        rows, cols = rows_of(image), cols_of(head)
        scores = dot(k_ref[rows, cols], q_ref[rows, cols], NT)
        slots[image, head] = len(slots) % 3
        score_ref[slots[image, head], pl.ds(0, SIZES[image]), pl.ds(0, SIZES[image])] = scores

    def unit(image, head):
        size, rows, cols = SIZES[image], rows_of(image), cols_of(head)
        width = STRIP_A or size
        for first in range(0, size, width):
            scores = score_ref[slots[image, head], pl.ds(0, size), pl.ds(first, width)]
            if image != 1:
                live_u = lax.broadcasted_iota(jnp.int32, (size, width), 0) < live[image]
                scores = jnp.where(live_u, scores, -1e30)
            weights = jnp.exp2((scores - jnp.max(scores, axis=0, keepdims=True)) * (SCALE * LOG2E))
            live_t = lax.broadcasted_iota(jnp.int32, (1, width), 1) + first < live[image]
            factor = jnp.where(live_t, 1.0 / jnp.sum(weights, axis=0, keepdims=True), 0.0)
            prob_refs[image][head, :, pl.ds(first, width)] = weights * factor
        total = jnp.sum(prob_refs[image][head], axis=1, keepdims=True)
        total_ref[rows, cols] = jnp.broadcast_to(total, (size, HS))
        summed = jnp.sum(total * v_ref[rows, cols].astype(jnp.float32), axis=0, keepdims=True)
        means[image, head] = summed / jnp.maximum(live[image], 1).astype(jnp.float32)

    def project(head):
        mean = jnp.concatenate([means[image, head] for image in range(IMG_DEV)] + [jnp.zeros((5, HS), jnp.float32)], axis=0)
        return dot(mean.astype(jnp.bfloat16), proj_ref[cols_of(head), :], NN)

    means, slots = {}, {}
    arrive(*((name, 0) for name in "qkv"))
    score(0, 0)
    score(0, 1)
    unit(0, 0)
    score(0, 2)
    unit(0, 1)
    arrive(*((name, image) for image in (1, 2) for name in "qkv"))
    score(1, 0)
    unit(0, 2)
    score(2, 0)
    unit(1, 0)
    score(1, 1)
    unit(2, 0)
    score(2, 1)
    arrive(("proj", 0))
    share_ref[...] = project(0)
    unit(1, 1)
    score(1, 2)
    unit(2, 1)
    score(2, 2)
    arrive(("proj", 1), ("proj", 2))
    share_ref[...] += project(1)
    unit(1, 2)
    unit(2, 2)
    share = share_ref[...] + project(2)
    arrive("grad")
    grad = grad_ref[...].astype(jnp.float32)
    held = jnp.concatenate([jnp.zeros((3, WIDTH), jnp.float32), grad, jnp.zeros((2, WIDTH), jnp.float32)], axis=0)
    for peer in range(PEERS):
        send_ref[peer] = (share[:, peer * WIDTH : (peer + 1) * WIDTH] + held).astype(jnp.bfloat16)


def grads_kernel(
    got_ref, segment_ref, q_ref, k_ref, v_ref, proj_ref, prob0_ref, prob1_ref, prob2_ref, total_ref,
    pooled_ref, dq_hbm, dk_hbm, dv_hbm,
    dq_ref, dk_ref, dv_ref, score_ref, sems,
):
    prob_refs = (prob0_ref, prob1_ref, prob2_ref)
    copies = []

    def send(image, *pairs):
        rows = rows_of(image)
        for src, dst in pairs:
            copy = pltpu.make_async_copy(src.at[rows], dst.at[rows], sems.at[len(copies)])
            copy.start()
            copies.append(copy)

    got = [got_ref[peer] for peer in range(PEERS)]
    gathered = jnp.concatenate(got, axis=1)
    divisor = [
        jnp.maximum(live_count(segment_ref, image), 1).astype(jnp.float32) for image in range(IMG_DEV)
    ]

    def project(head):
        return dot(gathered, proj_ref[cols_of(head), :], NT)

    def score(image, head):
        size, rows, cols = SIZES[image], rows_of(image), cols_of(head)
        width = STRIP_B or size
        grad = (summed[head][3 + image : 4 + image] / divisor[image]).astype(jnp.bfloat16).astype(jnp.float32)
        across = jnp.sum(v_ref[rows, cols].astype(jnp.float32) * (grad * SCALE), axis=1, keepdims=True)
        dv_ref[rows, cols] = (total_ref[rows, cols] * grad).astype(jnp.bfloat16)
        for first in range(0, size, width):
            prob = prob_refs[image][head, :, pl.ds(first, width)]
            delta = jnp.sum(prob * across, axis=0, keepdims=True)
            score_ref[head, pl.ds(0, size), pl.ds(first, width)] = (prob * (across - delta)).astype(jnp.bfloat16)

    def unit(image, head):
        size, rows, cols = SIZES[image], rows_of(image), cols_of(head)
        score_grad = score_ref[head, pl.ds(0, size), pl.ds(0, size)]
        dk_ref[rows, cols] = dot(score_grad, q_ref[rows, cols], NN).astype(jnp.bfloat16)
        dq_ref[rows, cols] = dot(score_grad, k_ref[rows, cols], TN).astype(jnp.bfloat16)

    summed = [project(0)]
    units = [(image, head) for image in ORDER for head in range(HEADS_DEV)]
    for at, (image, head) in enumerate(units):
        if at + 1 < HEADS_DEV:
            summed.append(project(at + 1))
        score(image, head)
        if at > 0:
            unit(*units[at - 1])
        if head == 0 and at > 0:
            send(units[at - 1][0], (dq_ref, dq_hbm), (dk_ref, dk_hbm), (dv_ref, dv_hbm))
        if at == HEADS_DEV:
            pooled = got[0].astype(jnp.float32)
            for piece in got[1:]:
                pooled += piece.astype(jnp.float32)
            pooled_ref[...] = pooled[:IMG_DEV].astype(jnp.bfloat16)
    unit(*units[-1])
    send(ORDER[2], (dq_ref, dq_hbm), (dk_ref, dk_hbm), (dv_ref, dv_hbm))
    for copy in copies:
        copy.wait()


def in_hbm(x):
    return pltpu.with_memory_space_constraint(x, pltpu.HBM)


def on_device(patch_queries, patch_keys, patch_values, out_proj, pool_grad, image_of_slot):
    segment = image_of_slot.reshape(SLOTS // 128, 128)
    here, anywhere = pl.BlockSpec(memory_space=pltpu.VMEM), pl.BlockSpec(memory_space=pl.ANY)
    patch = (SLOTS, WIDTH)
    bf16, f32 = jnp.bfloat16, jnp.float32
    kept_shapes = (
        ((SLOTS // 128, 128), jnp.int32), (patch, bf16), (patch, bf16), (patch, bf16), ((WIDTH, D), bf16),
        *(((HEADS_DEV, size, size), f32) for size in SIZES), (patch, f32),
    )
    send, *kept = pl.pallas_call(
        probs_kernel,
        out_shape=[pltpu.VMEM((PEERS, ROWS, WIDTH), bf16)] + [pltpu.VMEM(*s) for s in kept_shapes],
        in_specs=[anywhere] * 6,
        out_specs=[here] * 10,
        scratch_shapes=[
            pltpu.VMEM((IMG_DEV, WIDTH), bf16), pltpu.VMEM((ROWS, D), f32),
            pltpu.VMEM((3, max(SIZES), max(SIZES)), f32), pltpu.SemaphoreType.DMA((14,)),
        ],
        compiler_params=pltpu.CompilerParams(vmem_limit_bytes=VMEM_LIMIT),
        name="probs",
    )(*(in_hbm(x) for x in (segment, pool_grad, patch_queries, patch_keys, patch_values, out_proj)))
    got = lax.all_to_all(send, "heads", 0, 0, tiled=False)
    grad_shape = jax.ShapeDtypeStruct(patch, bf16)
    return pl.pallas_call(
        grads_kernel,
        out_shape=[jax.ShapeDtypeStruct((IMG_DEV, WIDTH), bf16)] + [grad_shape] * 3,
        in_specs=[here] * 10,
        out_specs=[here] + [anywhere] * 3,
        scratch_shapes=[pltpu.VMEM(patch, bf16)] * 3
        + [pltpu.VMEM((IMG_DEV, max(SIZES), max(SIZES)), bf16), pltpu.SemaphoreType.DMA((9,))],
        compiler_params=pltpu.CompilerParams(vmem_limit_bytes=VMEM_LIMIT),
        name="grads",
    )(got, *kept)


def solution(mesh):
    in_specs = (
        P("dp", "heads"),
        P("dp", "heads"),
        P("dp", "heads"),
        P("heads", None),
        P("dp", "heads"),
        P("dp"),
    )
    out_specs = (P("dp", "heads"), P("dp", "heads"), P("dp", "heads"), P("dp", "heads"))
    return jax.shard_map(
        on_device, mesh=mesh, in_specs=in_specs, out_specs=out_specs, check_vma=False
    )
```

```python
import functools

import jax
import jax.numpy as jnp
from jax import lax
from jax.experimental import pallas as pl
from jax.experimental.pallas import tpu as pltpu
from jax.sharding import PartitionSpec as P

HS = 128
D = 6144
HEADS_DEV = 3
WIDTH = HEADS_DEV * HS
PEERS = 16
SLOTS = 1024
IMG_DEV = 3
STARTS = (0, 256, 640)
SIZES = (256, 384, 384)
SCALE = HS**-0.5
LOG2E = 1.4426950408889634
ROWS = 8
STRIP_A = 128
STRIP_B = 0
ORDER = (1, 2, 0)
VMEM_LIMIT = 24 * 2**20

NT = (((1,), (1,)), ((), ()))
NN = (((1,), (0,)), ((), ()))
TN = (((0,), (0,)), ((), ()))


def dot(a, b, dims):
    return lax.dot_general(a, b, dims, preferred_element_type=jnp.float32)


def live_count(segment_ref, image):
    first, last = STARTS[image] // 128, (STARTS[image] + SIZES[image]) // 128
    live = (segment_ref[first:last, :] >= 0).astype(jnp.float32)
    return jnp.sum(live).astype(jnp.int32)


def rows_of(image):
    return pl.ds(STARTS[image], SIZES[image])


def cols_of(head):
    return pl.ds(head * HS, HS)


def probs_kernel(
    segment_hbm, grad_hbm, q_hbm, k_hbm, v_hbm, proj_hbm,
    send_ref, segment_ref, q_ref, k_ref, v_ref, proj_ref, prob0_ref, prob1_ref, prob2_ref, total_ref,
    grad_ref, share_ref, score_ref, sems,
):
    prob_refs = (prob0_ref, prob1_ref, prob2_ref)
    copies = {}

    def fetch(key, src, dst):
        copies[key] = pltpu.make_async_copy(src, dst, sems.at[len(copies)])
        copies[key].start()

    def arrive(*keys):
        for key in keys:
            copies[key].wait()

    fetch("segment", segment_hbm, segment_ref)
    for image in range(IMG_DEV):
        rows = rows_of(image)
        for name, src, dst in (("q", q_hbm, q_ref), ("k", k_hbm, k_ref), ("v", v_hbm, v_ref)):
            fetch((name, image), src.at[rows], dst.at[rows])
    fetch("grad", grad_hbm, grad_ref)
    for head in range(HEADS_DEV):
        rows = cols_of(head)
        fetch(("proj", head), proj_hbm.at[rows], proj_ref.at[rows])
    arrive("segment")
    live = [live_count(segment_ref, image) for image in range(IMG_DEV)]

    first_lane = lax.broadcasted_iota(jnp.int32, (max(SIZES), HS), 1) == 0
    slot = lax.broadcasted_iota(jnp.int32, (max(SIZES), HS), 0)
    ones = jnp.where(first_lane, 1.0, 0.0).astype(jnp.bfloat16)
    dead = {
        image: jnp.where(first_lane & (slot >= live[image]), -1e30, 0.0).astype(jnp.bfloat16)[: SIZES[image]]
        for image in (0, 2)
    }

    def score(image, head):
        rows, cols = rows_of(image), cols_of(head)
        keys, queries = k_ref[rows, cols], q_ref[rows, cols]
        if image != 1:
            keys = jnp.concatenate([keys, dead[image]], axis=1)
            queries = jnp.concatenate([queries, ones[: SIZES[image]]], axis=1)
        scores = dot(keys, queries, NT)
        slots[image, head] = len(slots) % 3
        score_ref[slots[image, head], pl.ds(0, SIZES[image]), pl.ds(0, SIZES[image])] = scores

    def unit(image, head):
        size, rows, cols = SIZES[image], rows_of(image), cols_of(head)
        width = STRIP_A or size
        for first in range(0, size, width):
            scores = score_ref[slots[image, head], pl.ds(0, size), pl.ds(first, width)]
            weights = jnp.exp2((scores - jnp.max(scores, axis=0, keepdims=True)) * (SCALE * LOG2E))
            live_t = lax.broadcasted_iota(jnp.int32, (1, width), 1) + first < live[image]
            factor = jnp.where(live_t, 1.0 / jnp.sum(weights, axis=0, keepdims=True), 0.0)
            prob_refs[image][head, :, pl.ds(first, width)] = weights * factor
        total = jnp.sum(prob_refs[image][head], axis=1, keepdims=True)
        total_ref[rows, cols] = jnp.broadcast_to(total, (size, HS))
        summed = jnp.sum(total * v_ref[rows, cols].astype(jnp.float32), axis=0, keepdims=True)
        means[image, head] = summed / jnp.maximum(live[image], 1).astype(jnp.float32)

    def project(head):
        mean = jnp.concatenate([means[image, head] for image in range(IMG_DEV)] + [jnp.zeros((5, HS), jnp.float32)], axis=0)
        return dot(mean.astype(jnp.bfloat16), proj_ref[cols_of(head), :], NN)

    means, slots = {}, {}
    arrive(*((name, 0) for name in "qkv"))
    score(0, 0)
    score(0, 1)
    unit(0, 0)
    score(0, 2)
    unit(0, 1)
    arrive(*((name, image) for image in (1, 2) for name in "qkv"))
    score(1, 0)
    unit(0, 2)
    score(2, 0)
    unit(1, 0)
    score(1, 1)
    unit(2, 0)
    score(2, 1)
    arrive(("proj", 0))
    share_ref[...] = project(0)
    unit(1, 1)
    score(1, 2)
    unit(2, 1)
    score(2, 2)
    arrive(("proj", 1))
    share_ref[...] += project(1)
    unit(1, 2)
    unit(2, 2)
    arrive(("proj", 2))
    share_ref[...] += project(2)
    arrive("grad")
    grad = grad_ref[...].astype(jnp.float32)
    grad = jnp.concatenate([grad[image : image + 1] for image in range(IMG_DEV)], axis=1)
    for peer in range(PEERS):
        share = [share_ref[pl.ds(image, 1), pl.ds(peer * WIDTH, WIDTH)] for image in range(IMG_DEV)]
        message = jnp.concatenate([jnp.concatenate(share, axis=1), grad], axis=0)
        send_ref[peer] = message.astype(jnp.bfloat16)


def grads_kernel(
    got_ref, segment_ref, q_ref, k_ref, v_ref, proj_ref, prob0_ref, prob1_ref, prob2_ref, total_ref,
    pooled_ref, dq_hbm, dk_hbm, dv_hbm,
    dq_ref, dk_ref, dv_ref, score_ref, gathered_ref, sems,
):
    prob_refs = (prob0_ref, prob1_ref, prob2_ref)
    copies = []

    def send(image, *pairs):
        rows = rows_of(image)
        for src, dst in pairs:
            copy = pltpu.make_async_copy(src.at[rows], dst.at[rows], sems.at[len(copies)])
            copy.start()
            copies.append(copy)

    got = [got_ref[peer].astype(jnp.float32) for peer in range(PEERS)]
    for peer in range(PEERS):
        for image in range(IMG_DEV):
            piece = got[peer][1:, image * WIDTH : (image + 1) * WIDTH]
            gathered_ref[pl.ds(image, 1), pl.ds(peer * WIDTH, WIDTH)] = piece
    gathered = gathered_ref[pl.ds(0, IMG_DEV), :].astype(jnp.bfloat16)
    divisor = [
        jnp.maximum(live_count(segment_ref, image), 1).astype(jnp.float32) for image in range(IMG_DEV)
    ]

    def project(head):
        return dot(gathered, proj_ref[cols_of(head), :], NT)

    def score(image, head):
        size, rows, cols = SIZES[image], rows_of(image), cols_of(head)
        width = STRIP_B or size
        grad = (summed[head][image : image + 1] / divisor[image]).astype(jnp.bfloat16).astype(jnp.float32)
        across = jnp.sum(v_ref[rows, cols].astype(jnp.float32) * (grad * SCALE), axis=1, keepdims=True)
        dv_ref[rows, cols] = (total_ref[rows, cols] * grad).astype(jnp.bfloat16)
        for first in range(0, size, width):
            prob = prob_refs[image][head, :, pl.ds(first, width)]
            delta = jnp.sum(prob * across, axis=0, keepdims=True)
            score_ref[head, pl.ds(0, size), pl.ds(first, width)] = (prob * (across - delta)).astype(jnp.bfloat16)

    def unit(image, head):
        size, rows, cols = SIZES[image], rows_of(image), cols_of(head)
        score_grad = score_ref[head, pl.ds(0, size), pl.ds(0, size)]
        dk_ref[rows, cols] = dot(score_grad, q_ref[rows, cols], NN).astype(jnp.bfloat16)
        dq_ref[rows, cols] = dot(score_grad, k_ref[rows, cols], TN).astype(jnp.bfloat16)

    summed = [project(0)]
    units = [(image, head) for image in ORDER for head in range(HEADS_DEV)]
    for at, (image, head) in enumerate(units):
        score(image, head)
        if at + 1 < HEADS_DEV:
            summed.append(project(at + 1))
        if at > 0:
            unit(*units[at - 1])
        if head == 0 and at > 0:
            send(units[at - 1][0], (dq_ref, dq_hbm), (dk_ref, dk_hbm), (dv_ref, dv_hbm))
        if at == HEADS_DEV:
            pooled = got[0][:1]
            for piece in got[1:]:
                pooled += piece[:1]
            pooled = jnp.concatenate([pooled[:, m * WIDTH : (m + 1) * WIDTH] for m in range(IMG_DEV)], axis=0)
            pooled_ref[...] = pooled.astype(jnp.bfloat16)
    unit(*units[-1])
    send(ORDER[2], (dq_ref, dq_hbm), (dk_ref, dk_hbm), (dv_ref, dv_hbm))
    for copy in copies:
        copy.wait()


def in_hbm(x):
    return pltpu.with_memory_space_constraint(x, pltpu.HBM)


def on_device(patch_queries, patch_keys, patch_values, out_proj, pool_grad, image_of_slot):
    segment = image_of_slot.reshape(SLOTS // 128, 128)
    here, anywhere = pl.BlockSpec(memory_space=pltpu.VMEM), pl.BlockSpec(memory_space=pl.ANY)
    patch = (SLOTS, WIDTH)
    bf16, f32 = jnp.bfloat16, jnp.float32
    kept_shapes = (
        ((SLOTS // 128, 128), jnp.int32), (patch, bf16), (patch, bf16), (patch, bf16), ((WIDTH, D), bf16),
        *(((HEADS_DEV, size, size), f32) for size in SIZES), (patch, f32),
    )
    send, *kept = pl.pallas_call(
        probs_kernel,
        out_shape=[pltpu.VMEM((PEERS, 2, IMG_DEV * WIDTH), bf16)] + [pltpu.VMEM(*s) for s in kept_shapes],
        in_specs=[anywhere] * 6,
        out_specs=[here] * 10,
        scratch_shapes=[
            pltpu.VMEM((IMG_DEV, WIDTH), bf16), pltpu.VMEM((ROWS, D), f32),
            pltpu.VMEM((3, max(SIZES), max(SIZES)), f32), pltpu.SemaphoreType.DMA((14,)),
        ],
        compiler_params=pltpu.CompilerParams(vmem_limit_bytes=VMEM_LIMIT),
        name="probs",
    )(*(in_hbm(x) for x in (segment, pool_grad, patch_queries, patch_keys, patch_values, out_proj)))
    got = lax.all_to_all(send, "heads", 0, 0, tiled=False)
    grad_shape = jax.ShapeDtypeStruct(patch, bf16)
    return pl.pallas_call(
        grads_kernel,
        out_shape=[jax.ShapeDtypeStruct((IMG_DEV, WIDTH), bf16)] + [grad_shape] * 3,
        in_specs=[here] * 10,
        out_specs=[here] + [anywhere] * 3,
        scratch_shapes=[pltpu.VMEM(patch, bf16)] * 3
        + [pltpu.VMEM((IMG_DEV, max(SIZES), max(SIZES)), bf16), pltpu.VMEM((ROWS, D), f32), pltpu.SemaphoreType.DMA((9,))],
        compiler_params=pltpu.CompilerParams(vmem_limit_bytes=VMEM_LIMIT),
        name="grads",
    )(got, *kept)


def solution(mesh):
    in_specs = (
        P("dp", "heads"),
        P("dp", "heads"),
        P("dp", "heads"),
        P("heads", None),
        P("dp", "heads"),
        P("dp"),
    )
    out_specs = (P("dp", "heads"), P("dp", "heads"), P("dp", "heads"), P("dp", "heads"))
    return jax.shard_map(
        on_device, mesh=mesh, in_specs=in_specs, out_specs=out_specs, check_vma=False
    )
```

```python
import functools

import jax
import jax.numpy as jnp
from jax import lax
from jax.experimental import pallas as pl
from jax.experimental.pallas import tpu as pltpu
from jax.sharding import PartitionSpec as P

HS = 128
D = 6144
HEADS_DEV = 3
WIDTH = HEADS_DEV * HS
PEERS = 16
SLOTS = 1024
IMG_DEV = 3
STARTS = (0, 256, 640)
SIZES = (256, 384, 384)
SCALE = HS**-0.5
LOG2E = 1.4426950408889634
ROWS = 8
STRIP_A = 128
STRIP_B = 0
ORDER = (1, 2, 0)
VMEM_LIMIT = 24 * 2**20

NT = (((1,), (1,)), ((), ()))
NN = (((1,), (0,)), ((), ()))
TN = (((0,), (0,)), ((), ()))


def dot(a, b, dims):
    return lax.dot_general(a, b, dims, preferred_element_type=jnp.float32)


def live_count(segment_ref, image):
    first, last = STARTS[image] // 128, (STARTS[image] + SIZES[image]) // 128
    live = (segment_ref[first:last, :] >= 0).astype(jnp.float32)
    return jnp.sum(live).astype(jnp.int32)


def rows_of(image):
    return pl.ds(STARTS[image], SIZES[image])


def cols_of(head):
    return pl.ds(head * HS, HS)


def probs_kernel(
    segment_hbm, grad_hbm, q_hbm, k_hbm, v_hbm, proj_hbm,
    send_ref, segment_ref, q_ref, k_ref, v_ref, proj_ref, prob0_ref, prob1_ref, prob2_ref, total_ref,
    grad_ref, share_ref, score_ref, sems,
):
    prob_refs = (prob0_ref, prob1_ref, prob2_ref)
    copies = {}

    def fetch(key, src, dst):
        copies[key] = pltpu.make_async_copy(src, dst, sems.at[len(copies)])
        copies[key].start()

    def arrive(*keys):
        for key in keys:
            copies[key].wait()

    fetch("segment", segment_hbm, segment_ref)
    for image in range(IMG_DEV):
        rows = rows_of(image)
        for name, src, dst in (("q", q_hbm, q_ref), ("k", k_hbm, k_ref), ("v", v_hbm, v_ref)):
            fetch((name, image), src.at[rows], dst.at[rows])
    fetch("grad", grad_hbm, grad_ref)
    for head in range(HEADS_DEV):
        rows = cols_of(head)
        fetch(("proj", head), proj_hbm.at[rows], proj_ref.at[rows])
    arrive("segment")
    live = [live_count(segment_ref, image) for image in range(IMG_DEV)]

    first_lane = lax.broadcasted_iota(jnp.int32, (max(SIZES), HS), 1) == 0
    slot = lax.broadcasted_iota(jnp.int32, (max(SIZES), HS), 0)
    ones = jnp.where(first_lane, 1.0, 0.0).astype(jnp.bfloat16)
    dead = {
        image: jnp.where(first_lane & (slot >= live[image]), -1e30, 0.0).astype(jnp.bfloat16)[: SIZES[image]]
        for image in (0, 2)
    }

    def score(image, head):
        rows, cols = rows_of(image), cols_of(head)
        keys, queries = k_ref[rows, cols], q_ref[rows, cols]
        if image != 1:
            keys = jnp.concatenate([keys, dead[image]], axis=1)
            queries = jnp.concatenate([queries, ones[: SIZES[image]]], axis=1)
        scores = dot(keys, queries, NT)
        slots[image, head] = len(slots) % 3
        score_ref[slots[image, head], pl.ds(0, SIZES[image]), pl.ds(0, SIZES[image])] = scores

    def unit(image, head):
        size, rows, cols = SIZES[image], rows_of(image), cols_of(head)
        width = STRIP_A or size
        total = jnp.zeros((size, HS), jnp.float32)
        for first in range(0, size, width):
            scores = score_ref[slots[image, head], pl.ds(0, size), pl.ds(first, width)]
            weights = jnp.exp2((scores - jnp.max(scores, axis=0, keepdims=True)) * (SCALE * LOG2E))
            live_t = lax.broadcasted_iota(jnp.int32, (1, width), 1) + first < live[image]
            factor = jnp.where(live_t, 1.0 / jnp.sum(weights, axis=0, keepdims=True), 0.0)
            prob = weights * factor
            prob_refs[image][head, :, pl.ds(first, width)] = prob
            total += prob
        total = jnp.sum(total, axis=1, keepdims=True)
        total_ref[rows, cols] = jnp.broadcast_to(total, (size, HS))
        summed = jnp.sum(total * v_ref[rows, cols].astype(jnp.float32), axis=0, keepdims=True)
        means[image, head] = summed / jnp.maximum(live[image], 1).astype(jnp.float32)

    def project(head):
        mean = jnp.concatenate([means[image, head] for image in range(IMG_DEV)] + [jnp.zeros((5, HS), jnp.float32)], axis=0)
        return dot(mean.astype(jnp.bfloat16), proj_ref[cols_of(head), :], NN)

    means, slots = {}, {}
    arrive(("q", 0), ("k", 0))
    score(0, 0)
    score(0, 1)
    arrive(("v", 0))
    unit(0, 0)
    score(0, 2)
    unit(0, 1)
    arrive(*((name, image) for image in (1, 2) for name in "qkv"))
    score(1, 0)
    unit(0, 2)
    score(2, 0)
    unit(1, 0)
    score(1, 1)
    unit(2, 0)
    score(2, 1)
    arrive(("proj", 0))
    share_ref[...] = project(0)
    unit(1, 1)
    score(1, 2)
    unit(2, 1)
    score(2, 2)
    arrive(("proj", 1))
    share_ref[...] += project(1)
    unit(1, 2)
    unit(2, 2)
    arrive(("proj", 2))
    share_ref[...] += project(2)
    arrive("grad")
    grad = grad_ref[...].astype(jnp.float32)
    grad = jnp.concatenate([grad[image : image + 1] for image in range(IMG_DEV)], axis=1)
    for peer in range(PEERS):
        share = [share_ref[pl.ds(image, 1), pl.ds(peer * WIDTH, WIDTH)] for image in range(IMG_DEV)]
        message = jnp.concatenate([jnp.concatenate(share, axis=1), grad], axis=0)
        send_ref[peer] = message.astype(jnp.bfloat16)


def grads_kernel(
    got_ref, segment_ref, q_ref, k_ref, v_ref, proj_ref, prob0_ref, prob1_ref, prob2_ref, total_ref,
    pooled_hbm, dq_hbm, dk_hbm, dv_hbm,
    pooled_ref, dq_ref, dk_ref, dv_ref, score_ref, gathered_ref, sems,
):
    prob_refs = (prob0_ref, prob1_ref, prob2_ref)
    copies = []

    def send(image, *pairs):
        rows = rows_of(image)
        for src, dst in pairs:
            copy = pltpu.make_async_copy(src.at[rows], dst.at[rows], sems.at[len(copies)])
            copy.start()
            copies.append(copy)

    pooled_copy = pltpu.make_async_copy(pooled_ref, pooled_hbm, sems.at[9])
    got = [got_ref[peer].astype(jnp.float32) for peer in range(PEERS)]
    for peer in range(PEERS):
        for image in range(IMG_DEV):
            piece = got[peer][1:, image * WIDTH : (image + 1) * WIDTH]
            gathered_ref[pl.ds(image, 1), pl.ds(peer * WIDTH, WIDTH)] = piece
    gathered = gathered_ref[pl.ds(0, IMG_DEV), :].astype(jnp.bfloat16)
    divisor = [
        jnp.maximum(live_count(segment_ref, image), 1).astype(jnp.float32) for image in range(IMG_DEV)
    ]

    def project(head):
        return dot(gathered, proj_ref[cols_of(head), :], NT)

    def score(image, head):
        size, rows, cols = SIZES[image], rows_of(image), cols_of(head)
        width = STRIP_B or size
        grad = (summed[head][image : image + 1] / divisor[image]).astype(jnp.bfloat16).astype(jnp.float32)
        across = jnp.sum(v_ref[rows, cols].astype(jnp.float32) * (grad * SCALE), axis=1, keepdims=True)
        dv_ref[rows, cols] = (total_ref[rows, cols] * grad).astype(jnp.bfloat16)
        for first in range(0, size, width):
            prob = prob_refs[image][head, :, pl.ds(first, width)]
            delta = jnp.sum(prob * across, axis=0, keepdims=True)
            score_ref[head, pl.ds(0, size), pl.ds(first, width)] = (prob * (across - delta)).astype(jnp.bfloat16)

    def unit(image, head):
        size, rows, cols = SIZES[image], rows_of(image), cols_of(head)
        score_grad = score_ref[head, pl.ds(0, size), pl.ds(0, size)]
        dk_ref[rows, cols] = dot(score_grad, q_ref[rows, cols], NN).astype(jnp.bfloat16)
        dq_ref[rows, cols] = dot(score_grad, k_ref[rows, cols], TN).astype(jnp.bfloat16)

    summed = [project(0)]
    units = [(image, head) for image in ORDER for head in range(HEADS_DEV)]
    for at, (image, head) in enumerate(units):
        score(image, head)
        if at + 1 < HEADS_DEV:
            summed.append(project(at + 1))
        if at > 0:
            unit(*units[at - 1])
        if head == 0 and at > 0:
            send(units[at - 1][0], (dq_ref, dq_hbm), (dk_ref, dk_hbm), (dv_ref, dv_hbm))
        if at == 0:
            pooled = got[0][:1]
            for piece in got[1:]:
                pooled += piece[:1]
            pooled = jnp.concatenate([pooled[:, m * WIDTH : (m + 1) * WIDTH] for m in range(IMG_DEV)], axis=0)
            pooled_ref[...] = pooled.astype(jnp.bfloat16)
            pooled_copy.start()
    send(ORDER[2], (dv_ref, dv_hbm))
    unit(*units[-1])
    send(ORDER[2], (dq_ref, dq_hbm), (dk_ref, dk_hbm))
    pooled_copy.wait()
    for copy in copies:
        copy.wait()


def in_hbm(x):
    return pltpu.with_memory_space_constraint(x, pltpu.HBM)


def on_device(patch_queries, patch_keys, patch_values, out_proj, pool_grad, image_of_slot):
    segment = image_of_slot.reshape(SLOTS // 128, 128)
    here, anywhere = pl.BlockSpec(memory_space=pltpu.VMEM), pl.BlockSpec(memory_space=pl.ANY)
    patch = (SLOTS, WIDTH)
    bf16, f32 = jnp.bfloat16, jnp.float32
    kept_shapes = (
        ((SLOTS // 128, 128), jnp.int32), (patch, bf16), (patch, bf16), (patch, bf16), ((WIDTH, D), bf16),
        *(((HEADS_DEV, size, size), f32) for size in SIZES), (patch, f32),
    )
    send, *kept = pl.pallas_call(
        probs_kernel,
        out_shape=[pltpu.VMEM((PEERS, 2, IMG_DEV * WIDTH), bf16)] + [pltpu.VMEM(*s) for s in kept_shapes],
        in_specs=[anywhere] * 6,
        out_specs=[here] * 10,
        scratch_shapes=[
            pltpu.VMEM((IMG_DEV, WIDTH), bf16), pltpu.VMEM((ROWS, D), f32),
            pltpu.VMEM((3, max(SIZES), max(SIZES)), f32), pltpu.SemaphoreType.DMA((14,)),
        ],
        compiler_params=pltpu.CompilerParams(vmem_limit_bytes=VMEM_LIMIT),
        name="probs",
    )(*(in_hbm(x) for x in (segment, pool_grad, patch_queries, patch_keys, patch_values, out_proj)))
    got = lax.all_to_all(send, "heads", 0, 0, tiled=False)
    grad_shape = jax.ShapeDtypeStruct(patch, bf16)
    return pl.pallas_call(
        grads_kernel,
        out_shape=[jax.ShapeDtypeStruct((IMG_DEV, WIDTH), bf16)] + [grad_shape] * 3,
        in_specs=[here] * 10,
        out_specs=[anywhere] * 4,
        scratch_shapes=[pltpu.VMEM((IMG_DEV, WIDTH), bf16)] + [pltpu.VMEM(patch, bf16)] * 3
        + [pltpu.VMEM((IMG_DEV, max(SIZES), max(SIZES)), bf16), pltpu.VMEM((ROWS, D), f32), pltpu.SemaphoreType.DMA((10,))],
        compiler_params=pltpu.CompilerParams(vmem_limit_bytes=VMEM_LIMIT),
        name="grads",
    )(got, *kept)


def solution(mesh):
    in_specs = (
        P("dp", "heads"),
        P("dp", "heads"),
        P("dp", "heads"),
        P("heads", None),
        P("dp", "heads"),
        P("dp"),
    )
    out_specs = (P("dp", "heads"), P("dp", "heads"), P("dp", "heads"), P("dp", "heads"))
    return jax.shard_map(
        on_device, mesh=mesh, in_specs=in_specs, out_specs=out_specs, check_vma=False
    )
```

```python
import functools

import jax
import jax.numpy as jnp
from jax import lax
from jax.experimental import pallas as pl
from jax.experimental.pallas import tpu as pltpu
from jax.sharding import PartitionSpec as P

HS = 128
D = 6144
HEADS_DEV = 3
WIDTH = HEADS_DEV * HS
PEERS = 16
SLOTS = 1024
IMG_DEV = 3
STARTS = (0, 256, 640)
SIZES = (256, 384, 384)
SCALE = HS**-0.5
LOG2E = 1.4426950408889634
ROWS = 8
STRIP_A = 128
STRIP_B = 0
ORDER = (1, 2, 0)
VMEM_LIMIT = 24 * 2**20

NT = (((1,), (1,)), ((), ()))
NN = (((1,), (0,)), ((), ()))
TN = (((0,), (0,)), ((), ()))


def dot(a, b, dims):
    return lax.dot_general(a, b, dims, preferred_element_type=jnp.float32)


def live_count(segment_ref, image):
    first, last = STARTS[image] // 128, (STARTS[image] + SIZES[image]) // 128
    live = (segment_ref[first:last, :] >= 0).astype(jnp.float32)
    return jnp.sum(live).astype(jnp.int32)


def rows_of(image):
    return pl.ds(STARTS[image], SIZES[image])


def cols_of(head):
    return pl.ds(head * HS, HS)


def enters_last():
    return (lax.axis_index("dp") == 0) & (lax.axis_index("heads") == 0)


def probs_kernel(
    segment_hbm, grad_hbm, q_hbm, k_hbm, v_hbm, proj_hbm,
    send_ref, segment_ref, q_ref, k_ref, v_ref, proj_ref, turned_ref, prob0_ref, prob1_ref, prob2_ref, total_ref,
    grad_ref, share_ref, score_ref, sems,
):
    prob_refs = (prob0_ref, prob1_ref, prob2_ref)
    copies = {}

    def fetch(key, src, dst):
        copies[key] = pltpu.make_async_copy(src, dst, sems.at[len(copies)])
        copies[key].start()

    def arrive(*keys):
        for key in keys:
            copies[key].wait()

    fetch("segment", segment_hbm, segment_ref)
    for image in range(IMG_DEV):
        rows = rows_of(image)
        for name, src, dst in (("q", q_hbm, q_ref), ("k", k_hbm, k_ref), ("v", v_hbm, v_ref)):
            fetch((name, image), src.at[rows], dst.at[rows])
    fetch("grad", grad_hbm, grad_ref)
    for head in range(HEADS_DEV):
        rows = cols_of(head)
        fetch(("proj", head), proj_hbm.at[rows], proj_ref.at[rows])
    arrive("segment")
    live = [live_count(segment_ref, image) for image in range(IMG_DEV)]

    first_lane = lax.broadcasted_iota(jnp.int32, (max(SIZES), HS), 1) == 0
    slot = lax.broadcasted_iota(jnp.int32, (max(SIZES), HS), 0)
    ones = jnp.where(first_lane, 1.0, 0.0).astype(jnp.bfloat16)
    dead = {
        image: jnp.where(first_lane & (slot >= live[image]), -1e30, 0.0).astype(jnp.bfloat16)[: SIZES[image]]
        for image in (0, 2)
    }

    def score(image, head):
        rows, cols = rows_of(image), cols_of(head)
        keys, queries = k_ref[rows, cols], q_ref[rows, cols]
        if image != 1:
            keys = jnp.concatenate([keys, dead[image]], axis=1)
            queries = jnp.concatenate([queries, ones[: SIZES[image]]], axis=1)
        scores = dot(keys, queries, NT)
        slots[image, head] = len(slots) % 3
        score_ref[slots[image, head], pl.ds(0, SIZES[image]), pl.ds(0, SIZES[image])] = scores

    def unit(image, head):
        size, rows, cols = SIZES[image], rows_of(image), cols_of(head)
        width = STRIP_A or size
        total = jnp.zeros((size, HS), jnp.float32)
        for first in range(0, size, width):
            scores = score_ref[slots[image, head], pl.ds(0, size), pl.ds(first, width)]
            weights = jnp.exp2((scores - jnp.max(scores, axis=0, keepdims=True)) * (SCALE * LOG2E))
            live_t = lax.broadcasted_iota(jnp.int32, (1, width), 1) + first < live[image]
            factor = jnp.where(live_t, 1.0 / jnp.sum(weights, axis=0, keepdims=True), 0.0)
            prob = weights * factor
            prob_refs[image][head, :, pl.ds(first, width)] = prob
            total += prob
        total = jnp.sum(total, axis=1, keepdims=True)
        total_ref[rows, cols] = jnp.broadcast_to(total, (size, HS))
        summed = jnp.sum(total * v_ref[rows, cols].astype(jnp.float32), axis=0, keepdims=True)
        means[image, head] = summed / jnp.maximum(live[image], 1).astype(jnp.float32)

    def project(head):
        mean = jnp.concatenate([means[image, head] for image in range(IMG_DEV)] + [jnp.zeros((5, HS), jnp.float32)], axis=0)
        return dot(mean.astype(jnp.bfloat16), proj_ref[cols_of(head), :], NN)

    means, slots = {}, {}
    arrive(("q", 0), ("k", 0))
    score(0, 0)
    score(0, 1)
    arrive(("v", 0))
    unit(0, 0)
    score(0, 2)
    unit(0, 1)
    arrive(*((name, image) for image in (1, 2) for name in "qkv"))
    score(1, 0)
    unit(0, 2)
    score(2, 0)
    unit(1, 0)
    score(1, 1)
    unit(2, 0)
    score(2, 1)
    arrive(("proj", 0))
    share_ref[...] = project(0)
    unit(1, 1)
    score(1, 2)
    unit(2, 1)
    score(2, 2)
    arrive(("proj", 1))
    share_ref[...] += project(1)
    unit(1, 2)
    unit(2, 2)
    arrive(("proj", 2))
    share_ref[...] += project(2)
    arrive("grad")
    grad = grad_ref[...].astype(jnp.float32)
    grad = jnp.concatenate([grad[image : image + 1] for image in range(IMG_DEV)], axis=1)
    for peer in range(PEERS):
        share = [share_ref[pl.ds(image, 1), pl.ds(peer * WIDTH, WIDTH)] for image in range(IMG_DEV)]
        message = jnp.concatenate([jnp.concatenate(share, axis=1), grad], axis=0)
        send_ref[peer] = message.astype(jnp.bfloat16)

    @pl.when(jnp.logical_not(enters_last()))
    def _():
        @pl.loop(0, PEERS)
        def _(peer):
            block = pl.ds(pl.multiple_of(peer * WIDTH, WIDTH), WIDTH)
            turned_ref[block, :] = jnp.transpose(proj_ref[:, block])


def grads_kernel(
    got_ref, segment_ref, q_ref, k_ref, v_ref, proj_ref, turned_ref, prob0_ref, prob1_ref, prob2_ref, total_ref,
    pooled_hbm, dq_hbm, dk_hbm, dv_hbm,
    pooled_ref, dq_ref, dk_ref, dv_ref, score_ref, gathered_ref, summed_ref, sems,
):
    prob_refs = (prob0_ref, prob1_ref, prob2_ref)
    copies = []

    def send(image, *pairs):
        rows = rows_of(image)
        for src, dst in pairs:
            copy = pltpu.make_async_copy(src.at[rows], dst.at[rows], sems.at[len(copies)])
            copy.start()
            copies.append(copy)

    pooled_copy = pltpu.make_async_copy(pooled_ref, pooled_hbm, sems.at[9])
    got = [got_ref[peer].astype(jnp.float32) for peer in range(PEERS)]
    for peer in range(PEERS):
        for image in range(IMG_DEV):
            piece = got[peer][1:, image * WIDTH : (image + 1) * WIDTH]
            gathered_ref[pl.ds(image, 1), pl.ds(peer * WIDTH, WIDTH)] = piece
    gathered = gathered_ref[pl.ds(0, IMG_DEV), :].astype(jnp.bfloat16)
    divisor = [
        jnp.maximum(live_count(segment_ref, image), 1).astype(jnp.float32) for image in range(IMG_DEV)
    ]

    @pl.when(enters_last())
    def _():
        summed_ref[...] = dot(gathered, proj_ref[...], NT)

    @pl.when(jnp.logical_not(enters_last()))
    def _():
        summed_ref[...] = dot(gathered, turned_ref[...], NN)

    def score(image, head):
        size, rows, cols = SIZES[image], rows_of(image), cols_of(head)
        width = STRIP_B or size
        grad = (summed_ref[pl.ds(image, 1), cols] / divisor[image]).astype(jnp.bfloat16).astype(jnp.float32)
        across = jnp.sum(v_ref[rows, cols].astype(jnp.float32) * (grad * SCALE), axis=1, keepdims=True)
        dv_ref[rows, cols] = (total_ref[rows, cols] * grad).astype(jnp.bfloat16)
        for first in range(0, size, width):
            prob = prob_refs[image][head, :, pl.ds(first, width)]
            delta = jnp.sum(prob * across, axis=0, keepdims=True)
            score_ref[head, pl.ds(0, size), pl.ds(first, width)] = (prob * (across - delta)).astype(jnp.bfloat16)

    def unit(image, head):
        size, rows, cols = SIZES[image], rows_of(image), cols_of(head)
        score_grad = score_ref[head, pl.ds(0, size), pl.ds(0, size)]
        dk_ref[rows, cols] = dot(score_grad, q_ref[rows, cols], NN).astype(jnp.bfloat16)
        dq_ref[rows, cols] = dot(score_grad, k_ref[rows, cols], TN).astype(jnp.bfloat16)

    units = [(image, head) for image in ORDER for head in range(HEADS_DEV)]
    for at, (image, head) in enumerate(units):
        score(image, head)
        if at > 0:
            unit(*units[at - 1])
        if head == 0 and at > 0:
            send(units[at - 1][0], (dq_ref, dq_hbm), (dk_ref, dk_hbm), (dv_ref, dv_hbm))
        if at == 0:
            pooled = got[0][:1]
            for piece in got[1:]:
                pooled += piece[:1]
            pooled = jnp.concatenate([pooled[:, m * WIDTH : (m + 1) * WIDTH] for m in range(IMG_DEV)], axis=0)
            pooled_ref[...] = pooled.astype(jnp.bfloat16)
            pooled_copy.start()
    send(ORDER[2], (dv_ref, dv_hbm))
    unit(*units[-1])
    send(ORDER[2], (dq_ref, dq_hbm), (dk_ref, dk_hbm))
    pooled_copy.wait()
    for copy in copies:
        copy.wait()


def in_hbm(x):
    return pltpu.with_memory_space_constraint(x, pltpu.HBM)


def on_device(patch_queries, patch_keys, patch_values, out_proj, pool_grad, image_of_slot):
    segment = image_of_slot.reshape(SLOTS // 128, 128)
    here, anywhere = pl.BlockSpec(memory_space=pltpu.VMEM), pl.BlockSpec(memory_space=pl.ANY)
    patch = (SLOTS, WIDTH)
    bf16, f32 = jnp.bfloat16, jnp.float32
    kept_shapes = (
        ((SLOTS // 128, 128), jnp.int32), (patch, bf16), (patch, bf16), (patch, bf16), ((WIDTH, D), bf16), ((D, WIDTH), bf16),
        *(((HEADS_DEV, size, size), f32) for size in SIZES), (patch, f32),
    )
    send, *kept = pl.pallas_call(
        probs_kernel,
        out_shape=[pltpu.VMEM((PEERS, 2, IMG_DEV * WIDTH), bf16)] + [pltpu.VMEM(*s) for s in kept_shapes],
        in_specs=[anywhere] * 6,
        out_specs=[here] * 11,
        scratch_shapes=[
            pltpu.VMEM((IMG_DEV, WIDTH), bf16), pltpu.VMEM((ROWS, D), f32),
            pltpu.VMEM((3, max(SIZES), max(SIZES)), f32), pltpu.SemaphoreType.DMA((14,)),
        ],
        compiler_params=pltpu.CompilerParams(vmem_limit_bytes=VMEM_LIMIT),
        name="probs",
    )(*(in_hbm(x) for x in (segment, pool_grad, patch_queries, patch_keys, patch_values, out_proj)))
    got = lax.all_to_all(send, "heads", 0, 0, tiled=False)
    grad_shape = jax.ShapeDtypeStruct(patch, bf16)
    return pl.pallas_call(
        grads_kernel,
        out_shape=[jax.ShapeDtypeStruct((IMG_DEV, WIDTH), bf16)] + [grad_shape] * 3,
        in_specs=[here] * 11,
        out_specs=[anywhere] * 4,
        scratch_shapes=[pltpu.VMEM((IMG_DEV, WIDTH), bf16)] + [pltpu.VMEM(patch, bf16)] * 3
        + [pltpu.VMEM((IMG_DEV, max(SIZES), max(SIZES)), bf16), pltpu.VMEM((ROWS, D), f32), pltpu.VMEM((IMG_DEV, WIDTH), f32),
           pltpu.SemaphoreType.DMA((10,))],
        compiler_params=pltpu.CompilerParams(vmem_limit_bytes=VMEM_LIMIT),
        name="grads",
    )(got, *kept)


def solution(mesh):
    in_specs = (
        P("dp", "heads"),
        P("dp", "heads"),
        P("dp", "heads"),
        P("heads", None),
        P("dp", "heads"),
        P("dp"),
    )
    out_specs = (P("dp", "heads"), P("dp", "heads"), P("dp", "heads"), P("dp", "heads"))
    return jax.shard_map(
        on_device, mesh=mesh, in_specs=in_specs, out_specs=out_specs, check_vma=False
    )
```

```python
import functools

import jax
import jax.numpy as jnp
from jax import lax
from jax.experimental import pallas as pl
from jax.experimental.pallas import tpu as pltpu
from jax.sharding import PartitionSpec as P

HS = 128
D = 6144
HEADS_DEV = 3
WIDTH = HEADS_DEV * HS
PEERS = 16
SLOTS = 1024
IMG_DEV = 3
STARTS = (0, 256, 640)
SIZES = (256, 384, 384)
SCALE = HS**-0.5
LOG2E = 1.4426950408889634
ROWS = 8
STRIP_A = 128
STRIP_B = 0
ORDER = (1, 2, 0)
VMEM_LIMIT = 24 * 2**20

NT = (((1,), (1,)), ((), ()))
NN = (((1,), (0,)), ((), ()))
TN = (((0,), (0,)), ((), ()))


def dot(a, b, dims):
    return lax.dot_general(a, b, dims, preferred_element_type=jnp.float32)


def live_count(segment_ref, image):
    first, last = STARTS[image] // 128, (STARTS[image] + SIZES[image]) // 128
    live = (segment_ref[first:last, :] >= 0).astype(jnp.float32)
    return jnp.sum(live).astype(jnp.int32)


def rows_of(image):
    return pl.ds(STARTS[image], SIZES[image])


def cols_of(head):
    return pl.ds(head * HS, HS)


def enters_last():
    return (lax.axis_index("dp") == 0) & (lax.axis_index("heads") == 0)


def probs_kernel(
    segment_hbm, grad_hbm, q_hbm, k_hbm, v_hbm, proj_hbm,
    send_ref, segment_ref, q_ref, k_ref, v_ref, proj_ref, turned_ref, prob0_ref, prob1_ref, prob2_ref, total_ref,
    grad_ref, share_ref, score_ref, sems,
):
    prob_refs = (prob0_ref, prob1_ref, prob2_ref)
    copies = {}

    def fetch(key, src, dst):
        copies[key] = pltpu.make_async_copy(src, dst, sems.at[len(copies)])
        copies[key].start()

    def arrive(*keys):
        for key in keys:
            copies[key].wait()

    fetch("segment", segment_hbm, segment_ref)
    for image in range(IMG_DEV):
        rows = rows_of(image)
        for name, src, dst in (("q", q_hbm, q_ref), ("k", k_hbm, k_ref), ("v", v_hbm, v_ref)):
            fetch((name, image), src.at[rows], dst.at[rows])
    fetch("grad", grad_hbm, grad_ref)
    for head in range(HEADS_DEV):
        rows = cols_of(head)
        fetch(("proj", head), proj_hbm.at[rows], proj_ref.at[rows])
    arrive("segment")
    live = [live_count(segment_ref, image) for image in range(IMG_DEV)]

    first_lane = lax.broadcasted_iota(jnp.int32, (max(SIZES), HS), 1) == 0
    slot = lax.broadcasted_iota(jnp.int32, (max(SIZES), HS), 0)
    ones = jnp.where(first_lane, 1.0, 0.0).astype(jnp.bfloat16)
    dead = {
        image: jnp.where(first_lane & (slot >= live[image]), -1e30, 0.0).astype(jnp.bfloat16)[: SIZES[image]]
        for image in (0, 2)
    }

    def score(image, head):
        rows, cols = rows_of(image), cols_of(head)
        keys, queries = k_ref[rows, cols], q_ref[rows, cols]
        if image != 1:
            keys = jnp.concatenate([keys, dead[image]], axis=1)
            queries = jnp.concatenate([queries, ones[: SIZES[image]]], axis=1)
        scores = dot(keys, queries, NT)
        slots[image, head] = len(slots) % 3
        score_ref[slots[image, head], pl.ds(0, SIZES[image]), pl.ds(0, SIZES[image])] = scores

    def unit(image, head):
        size, rows, cols = SIZES[image], rows_of(image), cols_of(head)
        width = STRIP_A or size
        total = jnp.zeros((size, HS), jnp.float32)
        for first in range(0, size, width):
            scores = score_ref[slots[image, head], pl.ds(0, size), pl.ds(first, width)]
            weights = jnp.exp2((scores - jnp.max(scores, axis=0, keepdims=True)) * (SCALE * LOG2E))
            live_t = lax.broadcasted_iota(jnp.int32, (1, width), 1) + first < live[image]
            factor = jnp.where(live_t, 1.0 / jnp.sum(weights, axis=0, keepdims=True), 0.0)
            prob = weights * factor
            prob_refs[image][head, :, pl.ds(first, width)] = prob
            total += prob
        total = jnp.sum(total, axis=1, keepdims=True)
        total_ref[rows, cols] = jnp.broadcast_to(total, (size, HS))
        summed = jnp.sum(total * v_ref[rows, cols].astype(jnp.float32), axis=0, keepdims=True)
        means[image, head] = summed / jnp.maximum(live[image], 1).astype(jnp.float32)

    def mean_of(head):
        rows = [means[image, head] for image in range(IMG_DEV)] + [jnp.zeros((5, HS), jnp.float32)]
        return jnp.concatenate(rows, axis=0).astype(jnp.bfloat16)

    def project(head, span=slice(None)):
        return dot(mean_of(head), proj_ref[cols_of(head), span], NN)

    means, slots = {}, {}
    arrive(("q", 0), ("k", 0))
    score(0, 0)
    score(0, 1)
    arrive(("v", 0))
    unit(0, 0)
    score(0, 2)
    unit(0, 1)
    arrive(*((name, image) for image in (1, 2) for name in "qkv"))
    score(1, 0)
    unit(0, 2)
    score(2, 0)
    unit(1, 0)
    score(1, 1)
    unit(2, 0)
    score(2, 1)
    unit(1, 1)
    score(1, 2)
    unit(2, 1)
    score(2, 2)
    arrive(("proj", 0), ("proj", 1))
    both = jnp.concatenate([mean_of(0), mean_of(1)], axis=1)
    share_ref[...] = dot(both, proj_ref[pl.ds(0, 2 * HS), :], NN)
    unit(1, 2)
    unit(2, 2)
    arrive(("proj", 2))
    arrive("grad")
    grad = grad_ref[...].astype(jnp.float32)
    grad = jnp.concatenate([grad[image : image + 1] for image in range(IMG_DEV)], axis=1)
    peers = PEERS // 4
    for part in range(4):
        span = pl.ds(part * peers * WIDTH, peers * WIDTH)
        share_ref[:, span] += project(2, span)
        for peer in range(part * peers, (part + 1) * peers):
            share = [share_ref[pl.ds(image, 1), pl.ds(peer * WIDTH, WIDTH)] for image in range(IMG_DEV)]
            message = jnp.concatenate([jnp.concatenate(share, axis=1), grad], axis=0)
            send_ref[peer] = message.astype(jnp.bfloat16)

    @pl.when(jnp.logical_not(enters_last()))
    def _():
        @pl.loop(0, PEERS)
        def _(peer):
            block = pl.ds(pl.multiple_of(peer * WIDTH, WIDTH), WIDTH)
            turned_ref[block, :] = jnp.transpose(proj_ref[:, block])


def grads_kernel(
    got_ref, segment_ref, q_ref, k_ref, v_ref, proj_ref, turned_ref, prob0_ref, prob1_ref, prob2_ref, total_ref,
    pooled_hbm, dq_hbm, dk_hbm, dv_hbm,
    pooled_ref, dq_ref, dk_ref, dv_ref, score_ref, gathered_ref, summed_ref, sems,
):
    prob_refs = (prob0_ref, prob1_ref, prob2_ref)
    copies = []

    def send(image, *pairs):
        rows = rows_of(image)
        for src, dst in pairs:
            copy = pltpu.make_async_copy(src.at[rows], dst.at[rows], sems.at[len(copies)])
            copy.start()
            copies.append(copy)

    pooled_copy = pltpu.make_async_copy(pooled_ref, pooled_hbm, sems.at[9])
    got = [got_ref[peer].astype(jnp.float32) for peer in range(PEERS)]
    for peer in range(PEERS):
        for image in range(IMG_DEV):
            piece = got[peer][1:, image * WIDTH : (image + 1) * WIDTH]
            gathered_ref[pl.ds(image, 1), pl.ds(peer * WIDTH, WIDTH)] = piece
    gathered = gathered_ref[pl.ds(0, IMG_DEV), :].astype(jnp.bfloat16)
    divisor = [
        jnp.maximum(live_count(segment_ref, image), 1).astype(jnp.float32) for image in range(IMG_DEV)
    ]

    @pl.when(enters_last())
    def _():
        summed_ref[...] = dot(gathered, proj_ref[...], NT)

    @pl.when(jnp.logical_not(enters_last()))
    def _():
        summed_ref[...] = dot(gathered, turned_ref[...], NN)

    def score(image, head):
        size, rows, cols = SIZES[image], rows_of(image), cols_of(head)
        width = STRIP_B or size
        grad = (summed_ref[pl.ds(image, 1), cols] / divisor[image]).astype(jnp.bfloat16).astype(jnp.float32)
        across = jnp.sum(v_ref[rows, cols].astype(jnp.float32) * (grad * SCALE), axis=1, keepdims=True)
        dv_ref[rows, cols] = (total_ref[rows, cols] * grad).astype(jnp.bfloat16)
        for first in range(0, size, width):
            prob = prob_refs[image][head, :, pl.ds(first, width)]
            delta = jnp.sum(prob * across, axis=0, keepdims=True)
            score_ref[head, pl.ds(0, size), pl.ds(first, width)] = (prob * (across - delta)).astype(jnp.bfloat16)

    def unit(image, head):
        size, rows, cols = SIZES[image], rows_of(image), cols_of(head)
        score_grad = score_ref[head, pl.ds(0, size), pl.ds(0, size)]
        dk_ref[rows, cols] = dot(score_grad, q_ref[rows, cols], NN).astype(jnp.bfloat16)
        dq_ref[rows, cols] = dot(score_grad, k_ref[rows, cols], TN).astype(jnp.bfloat16)

    units = [(image, head) for image in ORDER for head in range(HEADS_DEV)]
    for at, (image, head) in enumerate(units):
        score(image, head)
        if at > 0:
            unit(*units[at - 1])
        if head == 0 and at > 0:
            send(units[at - 1][0], (dq_ref, dq_hbm), (dk_ref, dk_hbm), (dv_ref, dv_hbm))
        if at == 0:
            pooled = got[0][:1]
            for piece in got[1:]:
                pooled += piece[:1]
            pooled = jnp.concatenate([pooled[:, m * WIDTH : (m + 1) * WIDTH] for m in range(IMG_DEV)], axis=0)
            pooled_ref[...] = pooled.astype(jnp.bfloat16)
            pooled_copy.start()
    send(ORDER[2], (dv_ref, dv_hbm))
    unit(*units[-1])
    send(ORDER[2], (dq_ref, dq_hbm), (dk_ref, dk_hbm))
    pooled_copy.wait()
    for copy in copies:
        copy.wait()


def in_hbm(x):
    return pltpu.with_memory_space_constraint(x, pltpu.HBM)


def on_device(patch_queries, patch_keys, patch_values, out_proj, pool_grad, image_of_slot):
    segment = image_of_slot.reshape(SLOTS // 128, 128)
    here, anywhere = pl.BlockSpec(memory_space=pltpu.VMEM), pl.BlockSpec(memory_space=pl.ANY)
    patch = (SLOTS, WIDTH)
    bf16, f32 = jnp.bfloat16, jnp.float32
    kept_shapes = (
        ((SLOTS // 128, 128), jnp.int32), (patch, bf16), (patch, bf16), (patch, bf16), ((WIDTH, D), bf16), ((D, WIDTH), bf16),
        *(((HEADS_DEV, size, size), f32) for size in SIZES), (patch, f32),
    )
    send, *kept = pl.pallas_call(
        probs_kernel,
        out_shape=[pltpu.VMEM((PEERS, 2, IMG_DEV * WIDTH), bf16)] + [pltpu.VMEM(*s) for s in kept_shapes],
        in_specs=[anywhere] * 6,
        out_specs=[here] * 11,
        scratch_shapes=[
            pltpu.VMEM((IMG_DEV, WIDTH), bf16), pltpu.VMEM((ROWS, D), f32),
            pltpu.VMEM((3, max(SIZES), max(SIZES)), f32), pltpu.SemaphoreType.DMA((14,)),
        ],
        compiler_params=pltpu.CompilerParams(vmem_limit_bytes=VMEM_LIMIT),
        name="probs",
    )(*(in_hbm(x) for x in (segment, pool_grad, patch_queries, patch_keys, patch_values, out_proj)))
    got = lax.all_to_all(send, "heads", 0, 0, tiled=False)
    grad_shape = jax.ShapeDtypeStruct(patch, bf16)
    return pl.pallas_call(
        grads_kernel,
        out_shape=[jax.ShapeDtypeStruct((IMG_DEV, WIDTH), bf16)] + [grad_shape] * 3,
        in_specs=[here] * 11,
        out_specs=[anywhere] * 4,
        scratch_shapes=[pltpu.VMEM((IMG_DEV, WIDTH), bf16)] + [pltpu.VMEM(patch, bf16)] * 3
        + [pltpu.VMEM((IMG_DEV, max(SIZES), max(SIZES)), bf16), pltpu.VMEM((ROWS, D), f32), pltpu.VMEM((IMG_DEV, WIDTH), f32),
           pltpu.SemaphoreType.DMA((10,))],
        compiler_params=pltpu.CompilerParams(vmem_limit_bytes=VMEM_LIMIT),
        name="grads",
    )(got, *kept)


def solution(mesh):
    in_specs = (
        P("dp", "heads"),
        P("dp", "heads"),
        P("dp", "heads"),
        P("heads", None),
        P("dp", "heads"),
        P("dp"),
    )
    out_specs = (P("dp", "heads"), P("dp", "heads"), P("dp", "heads"), P("dp", "heads"))
    return jax.shard_map(
        on_device, mesh=mesh, in_specs=in_specs, out_specs=out_specs, check_vma=False
    )
```
